32 devices in a mesh: cal: 2 (over x), gr: 4 (over y, core), gc: 4 (over z).
Axes of the slice: x: 2, y: 2, z: 4, core: 2. Of those that a mesh axis runs over, the one named last changes fastest.
Arguments:
- tokens: bfloat16 [512, 8192], P(('gr', 'gc'), 'cal'), may hold values from -12 to 12
- gate_weight: bfloat16 [8192, 28672], P(None, ('cal', 'gr', 'gc')), may hold values from -0.0625 to 0.0625
- up_weight: bfloat16 [8192, 28672], P(None, ('cal', 'gr', 'gc')), may hold values from -0.0625 to 0.0625
- hessian_slab: float32 [28672, 8192], P(('cal', 'gr'), 'gc'), may hold values from -1.2 to 1.2
- weight_error: float32 [512, 28672], P(None, ('cal', 'gr')), may hold values from -0.18 to 0.18
- slab_offset: int32 [1], replicated, may hold values from 0 to 20480
- token_count: int32 [1], replicated, may hold values from 512 to 1023
Outputs:
- new_slab: float32 [28672, 8192], P(('cal', 'gr'), 'gc')
- gradient: float32 [512, 8192], P(('cal', 'gr'), 'gc')
The draws below stay inside these ranges and needn't reach their ends.
Inputs may be any that keep to these rules, and one draw needn't show every extreme that they name: The slab holds the Hessian's columns slab_offset[0] to slab_offset[0] + 8191.
All inputs are finite; a program needn't handle non-finite values.
Results may differ from the reference program's by a relative error of at most 0.0038.
Values may be sent and summed in bfloat16 or wider, within the bound.
A program may use at most 192 MiB of HBM per device.

```python
import jax
import jax.numpy as jnp
from jax import lax

D = 8192
FF = 28672
SLAB = 8192
TOK = 512
ROWS = 512


def strengthened(values, key, source, target, parts, factor):
    owner, partner = [(jnp.arange(values.shape[axis_at]) // (values.shape[axis_at] // parts)).reshape([-1 if axis == axis_at else 1 for axis in range(values.ndim)]) for axis_at in (source, target)]
    chosen = jax.random.permutation(key, parts)[partner]
    strong = (owner == chosen) | (owner == (partner + parts // 2) % parts)
    return jnp.where(strong, factor * values, values)


def steps_of(rng, dims, pieces, smallest, largest):
    factor_of = 1.0
    for position, blocks in pieces:
        heights = jax.random.uniform(jax.random.fold_in(jax.random.fold_in(rng, 6), position), (blocks,), jnp.float32, smallest / len(pieces), largest / len(pieces))
        factor_of = factor_of * jnp.repeat(jnp.exp(heights), dims[position] // blocks).reshape((-1,) + (1,) * (len(dims) - 1 - position))
    return factor_of


def scatter_about(own_key, shape, spread, reach, cuts=(), dtype=jnp.bfloat16):
    entries = jax.random.normal(own_key, shape, jnp.float32) * spread
    if len(cuts) > 0:
        entries = steps_of(own_key, shape, cuts, -0.22, 0.18) * entries
    return jnp.clip(entries, min=-reach, max=reach).astype(dtype)


def heavy_noise(stream_key, dims, spread, limit, pieces, heavy, held_as=jnp.bfloat16):
    values = spread * jax.random.normal(stream_key, dims, jnp.float32)
    if pieces:
        values = values * steps_of(stream_key, dims, pieces, -0.22, 0.18)
    return jnp.clip(strengthened(values, jax.random.fold_in(stream_key, 3), *heavy), -limit, limit).astype(held_as)


def setup_inputs(seed: int = 0) -> dict:
    key_of = jax.random.split(jax.random.key(seed), 8)
    tokens = scatter_about(key_of[0], (TOK, D), 2.0, 12.0, ((0, 16), (1, 2)))
    gate_weight = scatter_about(key_of[1], (D, FF), D ** -0.5, 0.0625, ((1, 32),))
    up_weight = scatter_about(key_of[2], (D, FF), D ** -0.5, 0.0625, ((1, 32),))
    hessian_slab = scatter_about(key_of[3], (FF, SLAB), 0.2, 1.2, ((0, 8), (1, 4)), jnp.float32)
    weight_error = heavy_noise(key_of[4], (ROWS, FF), 0.03, 0.18, ((1, 8),), (1, 0, 8, 2.0), jnp.float32)
    slab_offset = jax.random.randint(key_of[5], (1,), 0, FF - SLAB + 1).astype(jnp.int32)
    token_count = jax.random.randint(key_of[6], (1,), TOK, 2 * TOK).astype(jnp.int32)
    return {"tokens": tokens, "gate_weight": gate_weight, "up_weight": up_weight, "hessian_slab": hessian_slab, "weight_error": weight_error, "slab_offset": slab_offset, "token_count": token_count}


def reference(tokens, gate_weight, up_weight, hessian_slab, weight_error, slab_offset, token_count):
    gate_pre = jnp.dot(tokens, gate_weight, preferred_element_type=jnp.float32)
    up_pre = jnp.dot(tokens, up_weight, preferred_element_type=jnp.float32)
    hidden = (jax.nn.silu(gate_pre) * up_pre).astype(jnp.bfloat16)
    first_col = slab_offset[0].astype(jnp.int32)
    window = lax.dynamic_slice_in_dim(hidden, first_col, SLAB, 1)
    gram = lax.dot_general(hidden, window, (((0,), (0,)), ((), ())), preferred_element_type=jnp.float32)
    new_slab = hessian_slab + gram / token_count[0].astype(jnp.float32)
    gradient = jnp.dot(weight_error, new_slab, precision=lax.Precision.HIGHEST, preferred_element_type=jnp.float32)
    return new_slab, gradient
```

```python
import functools

import jax
import jax.numpy as jnp
from jax import lax
from jax.experimental import pallas as pl
from jax.experimental.pallas import tpu as pltpu
from jax.sharding import PartitionSpec as P

MESH = pl.DeviceIdType.MESH
ANY = pl.BlockSpec(memory_space=pl.ANY)
VMEM = pl.BlockSpec(memory_space=pltpu.VMEM)


def place(dx, dy, dc):
    gr = lax.axis_index("gr")
    y, core = gr // 2, lax.rem(gr, 2)
    return (
        lax.rem(lax.axis_index("cal") + dx, 2),
        lax.rem(y + dy, 2) * 2 + lax.rem(core + dc, 2),
        lax.axis_index("gc"),
    )


def line_step(up):
    return (lax.axis_index("cal"), lax.axis_index("gr"), lax.axis_index("gc") + (1 if up else -1))


def greet(depth, partners, line):
    barrier = pltpu.get_barrier_semaphore()
    z = lax.axis_index("gc")
    for partner in partners:
        pl.semaphore_signal(barrier, inc=1, device_id=partner, device_id_type=MESH)
    if line:
        for up, there in ((True, z < depth - 1), (False, z > 0)):
            @pl.when(there)
            def _():
                pl.semaphore_signal(barrier, inc=1, device_id=line_step(up), device_id_type=MESH)
        both = jnp.where(z < depth - 1, 1, 0) + jnp.where(z > 0, 1, 0)
        pl.semaphore_wait(barrier, both + len(partners))
    else:
        pl.semaphore_wait(barrier, len(partners))


def line_events(depth):
    events = [(0, 0, None)]
    for d in range(1, depth):
        events += [(2 * d - 1, d, True), (2 * d, d, False)]
    return events


def here(depth, event):
    _, d, below = event
    z = lax.axis_index("gc")
    if below is None:
        return z >= 0, z
    if below:
        return z >= d, z - d
    return z + d < depth, z + d


def tokens_kernel(depth, x_ref, g_ref, own_sem, send, recv):
    rows, width = x_ref.shape
    z = lax.axis_index("gc")
    partners = [place(1, 0, 0), place(0, 1, 0), place(0, 0, 1)]
    x_next, y_next, sibling = partners
    greet(depth, partners, True)

    def block(where, origin, half=None):
        cal, gr, _ = where
        first = pl.multiple_of((gr * depth + origin) * rows, rows)
        count = rows
        if half is not None:
            count = rows // 2
            first = pl.multiple_of(first + half * count, count)
        return g_ref.at[pl.ds(first, count), pl.ds(pl.multiple_of(cal * width, width), width)]

    def copy(ref, target, kind, e, kind_there=None, e_there=None, src=None):
        return pltpu.make_async_remote_copy(
            src_ref=ref if src is None else src,
            dst_ref=ref,
            send_sem=send.at[kind, e],
            recv_sem=recv.at[kind, e if e_there is None else e_there],
            device_id=target,
            device_id_type=MESH,
        )

    mine = place(0, 0, 0)
    x_place, y_place, diag = place(1, 0, 0), place(0, 1, 0), place(1, 1, 0)
    events = line_events(depth)
    own = pltpu.make_async_copy(x_ref, block(mine, z), own_sem)
    own.start()

    def arrived(ref, kind, e):
        copy(ref, x_next, kind, e).wait_recv()

    def line_sends(event):
        e, d, below = event
        ok, origin = here(depth, event)
        src = x_ref if e == 0 else None
        out = []
        if below is not False:
            out.append((ok & (z < depth - 1), copy(block(mine, origin), line_step(True), 0, e, e_there=2 * d + 1, src=src)))
        if below is not True:
            out.append((ok & (z > 0), copy(block(mine, origin), line_step(False), 1, e, e_there=2 * d + 2, src=src)))
        return out

    def plane_sends(event):
        e = event[0]
        ok, origin = here(depth, event)
        src = x_ref if e == 0 else None
        ref = block(mine, origin)
        return [(ok, copy(ref, to, kind, e, src=src)) for kind, to in ((2, x_next), (3, y_next), (4, sibling))]

    def relay_sends(event):
        e = event[0]
        ok, origin = here(depth, event)
        return [
            (ok, copy(block(x_place, origin, 0), y_next, 5, e)),
            (ok, copy(block(x_place, origin), sibling, 7, e)),
        ], [
            (ok, copy(block(y_place, origin, 1), x_next, 6, e)),
            (ok, copy(block(y_place, origin), sibling, 8, e)),
        ]

    def diag_send(event):
        ok, origin = here(depth, event)
        return [(ok, copy(block(diag, origin), sibling, 9, event[0]))]

    def start(copies):
        for ok, c in copies:
            pl.when(ok)(c.start)

    count = len(events)
    for step in range(count + 2):
        if step < count:
            event = events[step]
            ok, origin = here(depth, event)
            if event[2] is not None:
                pl.when(ok)(lambda: arrived(block(mine, origin), 0 if event[2] else 1, event[0]))
            start(line_sends(event))
            start(plane_sends(event))
        if 1 <= step < count + 1:
            event = events[step - 1]
            ok, origin = here(depth, event)
            by_x, by_y = relay_sends(event)
            pl.when(ok)(lambda: arrived(block(x_place, origin), 2, event[0]))
            start(by_x)
            pl.when(ok)(lambda: arrived(block(y_place, origin), 3, event[0]))
            start(by_y)
        if step >= 2:
            event = events[step - 2]
            ok, origin = here(depth, event)
            pl.when(ok)(lambda: arrived(block(diag, origin, 0), 5, event[0]))
            pl.when(ok)(lambda: arrived(block(diag, origin, 1), 6, event[0]))
            start(diag_send(event))
    own.wait()
    for event in events:
        ok, origin = here(depth, event)
        for kind, at in ((4, (0, 0)), (7, (1, 0)), (8, (0, 1)), (9, (1, 1))):
            pl.when(ok)(lambda: arrived(block(place(*at, 1), origin), kind, event[0]))
        by_x, by_y = relay_sends(event)
        for there, c in line_sends(event) + plane_sends(event) + by_x + by_y + diag_send(event):
            pl.when(there)(c.wait_send)


def gather_tokens(tokens, depth):
    rows, width = tokens.shape
    events = 2 * depth + 1
    return pl.pallas_call(
        functools.partial(tokens_kernel, depth),
        out_shape=jax.ShapeDtypeStruct((rows * 4 * depth, width * 2), tokens.dtype),
        in_specs=[ANY],
        out_specs=ANY,
        scratch_shapes=[
            pltpu.SemaphoreType.DMA,
            pltpu.SemaphoreType.DMA((10, events)),
            pltpu.SemaphoreType.DMA((10, events)),
        ],
        compiler_params=pltpu.CompilerParams(collective_id=0, has_side_effects=True),
    )(tokens)


CHUNKS = 4
OTHERS = [(dx, dy, dc) for dx in (0, 1) for dy in (0, 1) for dc in (0, 1)][1:]


def flat(where):
    return where[0] * 4 + where[1]


def exchange(part_ref, got_ref, send, recv):
    rows = part_ref.shape[0] // 8
    copies = []
    for i, at in enumerate(OTHERS):
        to = place(*at)
        copies.append(
            pltpu.make_async_remote_copy(
                src_ref=part_ref.at[pl.ds(pl.multiple_of(flat(to) * rows, rows), rows), :],
                dst_ref=got_ref.at[i],
                send_sem=send.at[i],
                recv_sem=recv.at[i],
                device_id=to,
                device_id_type=MESH,
            )
        )
    return copies


def panel_kernel(depth, h_ref, part_ref, panel_ref, got_ref, own_sem, send, recv, psend, precv):
    total, width = h_ref.shape
    rows = total // CHUNKS
    z = lax.axis_index("gc")
    greet(depth, [place(*at) for at in OTHERS], True)
    events = line_events(depth)

    def block(origin, c):
        return panel_ref.at[pl.ds(c * rows, rows), pl.ds(pl.multiple_of(origin * width, width), width)]

    def copy(origin, c, up, e, e_there, src=None):
        return pltpu.make_async_remote_copy(
            src_ref=block(origin, c) if src is None else src,
            dst_ref=block(origin, c),
            send_sem=send.at[0 if up else 1, e, c],
            recv_sem=recv.at[0 if up else 1, e_there, c],
            device_id=line_step(up),
            device_id_type=MESH,
        )

    def sends(event, c):
        e, d, below = event
        ok, origin = here(depth, event)
        src = h_ref.at[pl.ds(c * rows, rows), :] if e == 0 else None
        out = []
        if below is not False:
            out.append((ok & (z < depth - 1), copy(origin, c, True, e, 2 * d + 1, src)))
        if below is not True:
            out.append((ok & (z > 0), copy(origin, c, False, e, 2 * d + 2, src)))
        return out

    own = pltpu.make_async_copy(h_ref, panel_ref.at[:, pl.ds(pl.multiple_of(z * width, width), width)], own_sem)
    for event in events:
        ok, origin = here(depth, event)
        for c in range(CHUNKS):
            if event[2] is not None:
                pl.when(ok)(copy(origin, c, event[2], 0, event[0]).wait_recv)
            for there, one in sends(event, c):
                pl.when(there)(one.start)
        if event[0] == 0:
            parts = exchange(part_ref, got_ref, psend, precv)
            for one in parts:
                one.start()
            own.start()
    own.wait()
    for one in parts:
        one.wait()
    for event in events:
        for c in range(CHUNKS):
            for there, one in sends(event, c):
                pl.when(there)(one.wait_send)


def gather_panel(hidden, part, depth):
    rows, width = hidden.shape
    events = 2 * depth + 1
    return pl.pallas_call(
        functools.partial(panel_kernel, depth),
        out_shape=(
            jax.ShapeDtypeStruct((rows, width * depth), hidden.dtype),
            jax.ShapeDtypeStruct((7, part.shape[0] // 8, part.shape[1]), part.dtype),
        ),
        in_specs=[ANY, ANY],
        out_specs=(ANY, ANY),
        scratch_shapes=[
            pltpu.SemaphoreType.DMA,
            pltpu.SemaphoreType.DMA((2, events, CHUNKS)),
            pltpu.SemaphoreType.DMA((2, events, CHUNKS)),
            pltpu.SemaphoreType.DMA((7,)),
            pltpu.SemaphoreType.DMA((7,)),
        ],
        compiler_params=pltpu.CompilerParams(collective_id=1, has_side_effects=True),
    )(hidden, part)


def window_kernel(share_ref, part_ref, window_ref, got_ref, land, send, recv, psend, precv):
    rows = share_ref.shape[0]
    half, quarter = rows // 2, rows // 4
    core = lax.rem(lax.axis_index("gr"), 2)
    x_next, y_next, sibling = place(1, 0, 0), place(0, 1, 0), place(0, 0, 1)
    greet(0, [place(*at) for at in OTHERS], False)

    def at(first, count):
        return pl.ds(pl.multiple_of(first, count), count)

    def copy(src, dst, i, to):
        return pltpu.make_async_remote_copy(
            src_ref=src, dst_ref=dst, send_sem=send.at[i], recv_sem=recv.at[i], device_id=to, device_id_type=MESH
        )

    def add(first, count, slot_first):
        mine = window_ref[at(first, count), :].astype(jnp.float32)
        other = land[pl.ds(slot_first, count), :].astype(jnp.float32)
        window_ref[at(first, count), :] = (mine + other).astype(window_ref.dtype)

    my, its = core * half, (1 - core) * half
    a, b = my, my + quarter
    first = copy(share_ref.at[at(its, half), :], land.at[pl.ds(0, half), :], 0, sibling)
    first.start()
    window_ref[at(my, half), :] = share_ref[at(my, half), :]
    first.wait_recv()
    add(my, half, 0)
    parts = exchange(part_ref, got_ref, psend, precv)
    s1 = copy(window_ref.at[at(a, quarter), :], land.at[pl.ds(half, quarter), :], 1, x_next)
    s2 = copy(window_ref.at[at(b, quarter), :], land.at[pl.ds(half + quarter, quarter), :], 2, y_next)
    s1.start()
    s2.start()
    for one in parts:
        one.start()
    s1.wait()
    add(a, quarter, half)
    s3 = copy(window_ref.at[at(a, quarter), :], land.at[pl.ds(2 * half, quarter), :], 3, y_next)
    s3.start()
    s2.wait()
    add(b, quarter, half + quarter)
    s4 = copy(window_ref.at[at(b, quarter), :], land.at[pl.ds(2 * half + quarter, quarter), :], 4, x_next)
    s4.start()
    s3.wait()
    add(a, quarter, 2 * half)
    s4.wait()
    add(b, quarter, 2 * half + quarter)
    last = copy(window_ref.at[at(my, half), :], window_ref.at[at(my, half), :], 5, sibling)
    last.start()
    first.wait_send()
    last.wait_send()
    copy(window_ref.at[at(its, half), :], window_ref.at[at(its, half), :], 5, sibling).wait_recv()
    for one in parts:
        one.wait()


def sum_window(share, part):
    rows, width = share.shape
    return pl.pallas_call(
        window_kernel,
        out_shape=(
            jax.ShapeDtypeStruct((rows, width), share.dtype),
            jax.ShapeDtypeStruct((7, part.shape[0] // 8, part.shape[1]), part.dtype),
        ),
        in_specs=[VMEM, ANY],
        out_specs=(VMEM, ANY),
        scratch_shapes=[
            pltpu.VMEM((3 * rows // 2, width), share.dtype),
            pltpu.SemaphoreType.DMA((6,)),
            pltpu.SemaphoreType.DMA((6,)),
            pltpu.SemaphoreType.DMA((7,)),
            pltpu.SemaphoreType.DMA((7,)),
        ],
        compiler_params=pltpu.CompilerParams(
            collective_id=2, has_side_effects=True, vmem_limit_bytes=24 * 1024 * 1024
        ),
    )(share, part)


def on_device(near, depth, tokens, gate_weight, up_weight, hessian_slab, weight_error, slab_offset, token_count):
    bf16, f32 = jnp.bfloat16, jnp.float32
    plane = ("cal", "gr")
    errors = weight_error.astype(bf16)
    plane_index = lax.axis_index("cal") * lax.axis_size("gr") + lax.axis_index("gr")

    def own_rows(part):
        count = part.shape[0] // (lax.axis_size("cal") * lax.axis_size("gr"))
        return lax.dynamic_slice_in_dim(part, plane_index * count, count, 0)

    if near:
        token_piece = gather_tokens(tokens, depth)
    else:
        token_rows = lax.all_gather(tokens, "cal", axis=1, tiled=True)
        token_piece = lax.all_gather(token_rows, ("gr", "gc"), axis=0, tiled=True)
    slab_part = jnp.dot(errors, hessian_slab.astype(bf16), preferred_element_type=f32)
    gate_pre = jnp.dot(token_piece, gate_weight, preferred_element_type=f32)
    up_pre = jnp.dot(token_piece, up_weight, preferred_element_type=f32)
    hidden = (jax.nn.silu(gate_pre) * up_pre).astype(bf16)
    if near:
        row_panel, slab_parts = gather_panel(hidden, slab_part, depth)
        slab_sum = own_rows(slab_part) + slab_parts.sum(0)
    else:
        row_panel = lax.all_gather(hidden, "gc", axis=1, tiled=True)
        slab_sum = lax.psum_scatter(slab_part, plane, scatter_dimension=0, tiled=True)
    panel_width = row_panel.shape[1]
    block_width = hessian_slab.shape[1]
    first_col = slab_offset[0] + lax.axis_index("gc") * block_width
    padded = jnp.pad(row_panel, ((0, 0), (block_width, block_width)))
    shifted = jnp.clip(
        first_col - plane_index * panel_width + block_width, 0, panel_width + block_width
    )
    own_share = lax.dynamic_slice_in_dim(padded, shifted, block_width, 1)
    mixed = lax.dot_general(errors, row_panel, (((1,), (1,)), ((), ())), preferred_element_type=f32)
    if near:
        window, mixed_parts = sum_window(own_share, mixed)
        mixed_sum = own_rows(mixed) + mixed_parts.sum(0)
    else:
        window = lax.psum(own_share, plane).astype(f32).astype(bf16)
        mixed_sum = lax.psum_scatter(mixed, plane, scatter_dimension=0, tiled=True)
    count = token_count[0].astype(f32)
    gram_block = lax.dot_general(
        row_panel, window, (((0,), (0,)), ((), ())), preferred_element_type=f32
    )
    new_slab = hessian_slab + gram_block / count
    gradient = slab_sum + jnp.dot(
        mixed_sum, window.astype(f32), precision=lax.Precision.HIGHEST, preferred_element_type=f32
    ) / count
    return (new_slab, gradient)


def solution(mesh):
    in_specs = (
        P(("gr", "gc"), "cal"),
        P(None, ("cal", "gr", "gc")),
        P(None, ("cal", "gr", "gc")),
        P(("cal", "gr"), "gc"),
        P(None, ("cal", "gr")),
        P(),
        P(),
    )
    out_specs = (P(("cal", "gr"), "gc"), P(("cal", "gr"), "gc"))
    near = mesh.shape["cal"] == 2 and mesh.shape["gr"] == 4
    return jax.shard_map(
        functools.partial(on_device, near, mesh.shape["gc"]),
        mesh=mesh, in_specs=in_specs, out_specs=out_specs, check_vma=False,
    )
```
